32 devices in a mesh: rows: 8 (over z, y), samples: 4 (over x, core).
Axes of the slice: x: 2, y: 2, z: 4, core: 2. Of those that a mesh axis runs over, the one named last changes fastest.
Arguments:
- matrix_block: bfloat16 [8192, 10240], P('rows', 'samples'), may hold values from -6 to 6
- sketch_matrix: bfloat16 [10240, 384], P('samples'), may hold values from -0.0625 to 0.0625
- local_pivots: int32 [8, 3, 256], P('rows'), may hold values from 0 to 511, as said below
- upper_pivots: int32 [6, 256], replicated, may hold values from 0 to 511, as said below
Outputs:
- leaf_basis: float32 [8192, 384], P(('rows', 'samples'))
- device_basis: float32 [4096, 384], P('rows')
- inner_basis: float32 [4096, 384], P('rows')
The draws below stay inside these ranges and needn't reach their ends.
Inputs may be any that keep to these rules, and one draw needn't show every extreme that they name: `local_pivots`: each row holds 256 distinct indices. `upper_pivots`: each row holds 256 distinct indices.
All inputs are finite; a program needn't handle non-finite values.
Results may differ from the reference program's by a relative error of at most 0.0003.
Values sent between devices are 32-bit elements; how exact they have to be, the bound alone decides.
No kernel may reach another device: no remote copies, remote signals or barrier semaphores. Data moves between devices by JAX's collectives and lax.ppermute only.
A program may use at most 128 MiB of HBM per device.

```python
import math
import jax
import jax.numpy as jnp
from jax import lax

LEAF = 512
RANK = 256
SKETCH = 384
CLUSTERS = 8
ROWS = 8192
COLS = 10240


def pivot_rows(key, row_count):
    keys = jax.random.split(key, row_count)

    def one_row(one_key):
        return jax.random.permutation(one_key, LEAF)[:RANK]
    return jax.vmap(one_row)(keys).astype(jnp.int32)


def draw_local_pivots(key, part):
    return pivot_rows(jax.random.fold_in(key, 11), CLUSTERS * 3).reshape(CLUSTERS, 3, RANK)


def draw_upper_pivots(key, part):
    return pivot_rows(jax.random.fold_in(key, 23), CLUSTERS - 2)


def level_of(rng, dims, pieces, low, top_value):
    def one(dim, blocks):
        steps = jax.random.uniform(jax.random.fold_in(jax.random.fold_in(rng, 6), dim), (blocks,), jnp.float32, low / len(pieces), top_value / len(pieces))
        return jnp.repeat(jnp.exp(steps), dims[dim] // blocks).reshape((-1,) + (1,) * (len(dims) - dim - 1))

    factor_of = one(*pieces[0])
    for cut in pieces[1:]:
        factor_of = factor_of * one(*cut)
    return factor_of


def noise(own_key, shape, deviation, reach, pieces=(), held_as=jnp.bfloat16):
    entries = deviation * jax.random.normal(own_key, shape, jnp.float32)
    if pieces:
        entries = entries * level_of(own_key, shape, pieces, -0.22, 0.18)
    return jnp.clip(entries, -reach, reach).astype(held_as)


def setup_inputs(seed: int = 0) -> dict:
    arg_keys = jax.random.split(jax.random.key(seed), 5)
    matrix_block = noise(arg_keys[0], (ROWS, COLS), 1.0, 6.0, ((0, 8), (1, 4)))
    sketch_matrix = noise(arg_keys[1], (COLS, SKETCH), COLS ** -0.5, 0.0625, ((0, 4),))
    local_pivots = draw_local_pivots(jax.random.fold_in(arg_keys[4], 71), 0)
    upper_pivots = draw_upper_pivots(jax.random.fold_in(arg_keys[4], 71), 0)
    return {"matrix_block": matrix_block, "sketch_matrix": sketch_matrix, "local_pivots": local_pivots, "upper_pivots": upper_pivots}


def basis_of(stacked):
    gram_matrix = jnp.dot(stacked.T.astype(jnp.float32), stacked.astype(jnp.float32), precision=lax.Precision.HIGHEST, preferred_element_type=jnp.float32)
    lower_factor = jnp.linalg.cholesky(gram_matrix)
    solved = jax.scipy.linalg.solve_triangular(lower_factor, stacked.T, lower=True)
    return solved.T * math.sqrt(LEAF)

def select_rows(matrix_rows, indices):
    return jnp.take(matrix_rows, indices, axis=0)

def reference(matrix_block, sketch_matrix, local_pivots, upper_pivots):
    sketch_wide = sketch_matrix.astype(jnp.float32)

    def leaf_samples(block_rows):
        return jnp.dot(block_rows.astype(jnp.float32), sketch_wide, precision=lax.Precision.HIGHEST)
    sketch_product = lax.map(leaf_samples, matrix_block.reshape(2 * CLUSTERS, LEAF, COLS))
    leaf_basis = lax.map(basis_of, sketch_product).reshape(2 * CLUSTERS * LEAF, SKETCH)
    leaf_pivots = local_pivots[:, :2].reshape(2 * CLUSTERS, RANK)
    skeleton = jax.vmap(select_rows)(sketch_product, leaf_pivots)
    stacked = skeleton.reshape(CLUSTERS, 2 * RANK, SKETCH)
    device_basis = lax.map(basis_of, stacked).reshape(CLUSTERS * LEAF, SKETCH)
    current = jax.vmap(select_rows)(stacked, local_pivots[:, 2])
    tree_depth = CLUSTERS.bit_length() - 1
    level_bases = []
    for height in range(1, tree_depth + 1):
        node_count = current.shape[0] // 2
        stacked = current.reshape(node_count, 2 * RANK, SKETCH)
        level_bases.append(lax.map(basis_of, stacked))
        if height < tree_depth:
            first_row = 2 ** (tree_depth - height) - 2
            current = jax.vmap(select_rows)(stacked, upper_pivots[first_row:first_row + node_count])
    blocks_out = []
    for device_index in range(CLUSTERS):
        if device_index == 0:
            height = tree_depth
        else:
            height = (device_index & -device_index).bit_length()
        blocks_out.append(level_bases[height - 1][device_index >> height])
    inner_basis = jnp.concatenate(blocks_out, 0)
    return (leaf_basis, device_basis, inner_basis)
```

```python
import functools
import math

import jax
import jax.numpy as jnp
from jax import lax
from jax.experimental import pallas as pl
from jax.experimental.pallas import tpu as pltpu
from jax.sharding import PartitionSpec as P

F32 = jnp.float32
BF16 = jnp.bfloat16
PANEL = 128
STRIP = 32
AHEAD = 5


def dot_of(left, right, left_dim, right_dim):
    return lax.dot_general(
        left, right, (((left_dim,), (right_dim,)), ((), ())), preferred_element_type=F32
    )


def halves(value):
    high = value.astype(BF16)
    return high, (value - high.astype(F32)).astype(BF16)


def dot3(left, right, left_dim, right_dim):
    left_high, left_low = halves(left)
    right_high, right_low = halves(right)
    cross = dot_of(left_high, right_low, left_dim, right_dim)
    cross += dot_of(left_low, right_high, left_dim, right_dim)
    return dot_of(left_high, right_high, left_dim, right_dim) + cross


def spread_row(tile, row):
    return jnp.broadcast_to(tile[row : row + 1], tile.shape)


def spread_lane(tile, lane):
    return jnp.broadcast_to(tile[:, lane : lane + 1], tile.shape)


def eliminate(strips, first, width):
    tiles = STRIP // 8
    lane = lax.broadcasted_iota(jnp.int32, (8, width), 1)
    sub = lax.broadcasted_iota(jnp.int32, (8, width), 0)
    rows = [[strip[8 * t : 8 * t + 8] for t in range(tiles)] for strip in strips]
    pivots = [[None] * tiles for _ in strips]
    columns = [
        {k: {t: spread_lane(own[t], first + k) for t in range(tiles)} for k in range(AHEAD + 1)}
        for own in rows
    ]
    for j in range(STRIP):
        at, row = j // 8, j % 8
        below = sub > row
        here = lane == first + j
        for own, ahead, seen in zip(rows, columns, pivots):
            column = ahead.pop(j)
            pivot = spread_row(column[at], row)
            seen[at] = pivot if row == 0 else jnp.where(sub >= row, pivot, seen[at])
            inverse = pl.reciprocal(pivot, approx=True)
            factor = {t: column[t] for t in range(at + 1, tiles)}
            if row < 7:
                factor[at] = jnp.where(below, column[at], 0.0)
            for later in ahead.values():
                value = spread_row(later[at], row)
                for t in later:
                    if t in factor:
                        later[t] = later[t] - (factor[t] * value) * inverse
            pivot_row = jnp.where(here, 1.0, spread_row(own[at], row)) * inverse
            for t in factor:
                cleared = jnp.logical_and(here, below) if t == at else here
                own[t] = jnp.where(cleared, 0.0, own[t]) - factor[t] * pivot_row
            new = j + AHEAD + 1
            if new < STRIP:
                ahead[new] = {
                    t: spread_lane(own[t], first + new) for t in range((j + 1) // 8, tiles)
                }
    scaled = []
    for own, seen in zip(rows, pivots):
        out = []
        for t in range(tiles):
            offset = lane - first - 8 * t
            tile = jnp.where(offset == sub, 1.0, own[t])
            tile = jnp.where(jnp.logical_and(offset > sub, lane < first + STRIP), 0.0, tile)
            out.append(tile * lax.rsqrt(seen[t]))
        scaled.append(jnp.concatenate(out, 0))
    return scaled


def panel_inverses(panels):
    width = panels[0].shape[0]
    rest = list(panels)
    inverse_rows = [[] for _ in panels]
    for first in range(0, width, STRIP):
        past = first + STRIP
        strips = eliminate([one[:STRIP] for one in rest], first, width)
        lane = lax.broadcasted_iota(jnp.int32, (STRIP, width), 1)
        for m, strip in enumerate(strips):
            inverse_rows[m].append(jnp.where(lane < past, strip, 0.0))
            if past < width:
                update = dot3(strip, strip, 0, 0)[past:]
                below = rest[m][STRIP:]
                lanes = lax.broadcasted_iota(jnp.int32, below.shape, 1)
                done = jnp.logical_and(lanes >= first, lanes < past)
                rest[m] = jnp.where(done, 0.0, below) - update
    return [jnp.concatenate(parts, 0) for parts in inverse_rows]


def basis_kernel(*refs, count):
    stacked, bases = refs[:count], refs[count : 2 * count]
    grams, left = refs[2 * count : 3 * count], refs[3 * count :]
    rows, columns = stacked[0].shape
    scale = math.sqrt(rows)
    for source, gram in zip(stacked, grams):
        value = source[...]
        gram[...] = dot3(value, value, 0, 0)
    for start in range(0, columns, PANEL):
        own, after = slice(start, start + PANEL), slice(start + PANEL, columns)
        last = start + PANEL == columns
        inverses = panel_inverses([gram[own, own] for gram in grams])
        for inverse, source, gram, basis, rest in zip(inverses, stacked, grams, bases, left):
            held = source if start == 0 else rest
            if not last:
                lower = dot3(gram[after, own], inverse, 1, 1)
                gram[after, after] = gram[after, after] - dot3(lower, lower, 1, 1)
            block = dot3(held[:, own], inverse, 1, 1)
            basis[:, own] = block * scale
            if not last:
                rest[:, after] = held[:, after] - dot3(block, lower, 1, 1)


def bases_of(stacked):
    count = len(stacked)
    rows, columns = stacked[0].shape
    vmem = pl.BlockSpec(memory_space=pltpu.VMEM)
    shape = jax.ShapeDtypeStruct((rows, columns), F32)
    return pl.pallas_call(
        functools.partial(basis_kernel, count=count),
        out_shape=[shape] * count,
        in_specs=[vmem] * count,
        out_specs=[vmem] * count,
        scratch_shapes=[pltpu.VMEM((columns, columns), F32)] * count
        + [pltpu.VMEM((rows, columns), F32)] * count,
        compiler_params=pltpu.CompilerParams(vmem_limit_bytes=48 << 20),
        name="bases",
    )(*stacked)


def partner_2(block, axis, bit):
    count = lax.axis_size(axis)
    route = []
    for low in range(count):
        high = low | 1 << bit
        if high != low and high < count:
            route += [(low, high), (high, low)]
    return lax.ppermute(block, axis, route)


def select_rows(matrix_rows, indices):
    return jnp.take(matrix_rows, indices, axis=0)


def climb_tree(current, tree_depth, position, upper_pivots):
    chosen = None
    for height in range(1, tree_depth + 1):
        partner = partner_2(current, "rows", height - 1)
        on_right = position >> height - 1 & 1 == 1
        left_part = jnp.where(on_right, partner, current)
        right_part = jnp.where(on_right, current, partner)
        stacked = jnp.concatenate([left_part, right_part], 0)
        low_bits = position & (1 << height) - 1
        is_owner = low_bits == 1 << height - 1
        if height == tree_depth:
            is_owner = jnp.logical_or(is_owner, position == 0)
        chosen = stacked if chosen is None else jnp.where(is_owner, stacked, chosen)
        if height < tree_depth:
            node_row = (1 << tree_depth - height) + (position >> height) - 2
            indices = lax.dynamic_index_in_dim(upper_pivots, node_row, 0, keepdims=False)
            current = select_rows(stacked, indices)
    return chosen


def on_device(matrix_block, sketch_matrix, local_pivots, upper_pivots):
    leaf_rows = matrix_block.shape[0] // 2
    partial_value = jnp.dot(matrix_block, sketch_matrix, preferred_element_type=jnp.float32)
    pivots = local_pivots[0]
    summed = lax.psum(partial_value, "samples")
    first_leaf = summed[:leaf_rows]
    second_leaf = summed[leaf_rows:]
    skeleton_a = select_rows(first_leaf, pivots[0])
    skeleton_b = select_rows(second_leaf, pivots[1])
    stacked = jnp.concatenate([skeleton_a, skeleton_b], 0)
    current = select_rows(stacked, pivots[2])
    tree_depth = lax.axis_size("rows").bit_length() - 1
    position = lax.axis_index("rows")
    node = climb_tree(current, tree_depth, position, upper_pivots)

    share = lax.axis_index("samples")
    shares = lax.axis_size("samples")
    second_half = share >= shares // 2
    own_leaf = jnp.where(second_half, second_leaf, first_leaf)
    leaf_basis, device_out, node_out = bases_of([own_leaf, stacked, node])
    share_rows = 2 * leaf_rows // shares
    leaf_out = lax.dynamic_slice_in_dim(
        leaf_basis, share % (shares // 2) * share_rows, share_rows, 0
    )
    return (leaf_out, device_out, node_out)


def solution(mesh):
    in_specs = (P("rows", "samples"), P("samples", None), P("rows", None, None), P())
    out_specs = (P(("rows", "samples"), None), P("rows", None), P("rows", None))
    return jax.shard_map(
        on_device, mesh=mesh, in_specs=in_specs, out_specs=out_specs, check_vma=False
    )
```

```python
import functools
import math

import jax
import jax.numpy as jnp
from jax import lax
from jax.experimental import pallas as pl
from jax.experimental.pallas import tpu as pltpu
from jax.sharding import PartitionSpec as P

F32 = jnp.float32
BF16 = jnp.bfloat16
PANEL = 128
STRIP = 32
AHEAD = 5
PRODUCT_VMEM = 61 << 20
SMALL_VMEM = 12 << 20
BASES_VMEM = 24 << 20
VMEM = pl.BlockSpec(memory_space=pltpu.VMEM)
SMEM = pl.BlockSpec(memory_space=pltpu.SMEM)


def dot_of(left, right, left_dim, right_dim):
    return lax.dot_general(
        left, right, (((left_dim,), (right_dim,)), ((), ())), preferred_element_type=F32
    )


def halves(value):
    high = value.astype(BF16)
    return high, (value - high.astype(F32)).astype(BF16)


def dot3(left, right, left_dim, right_dim):
    left_high, left_low = halves(left)
    right_high, right_low = halves(right)
    cross = dot_of(left_high, right_low, left_dim, right_dim)
    cross += dot_of(left_low, right_high, left_dim, right_dim)
    return dot_of(left_high, right_high, left_dim, right_dim) + cross


def spread_row(tile, row):
    return jnp.broadcast_to(tile[row : row + 1], tile.shape)


def spread_lane(tile, lane):
    return jnp.broadcast_to(tile[:, lane : lane + 1], tile.shape)


def eliminate(strips, first, width):
    tiles = STRIP // 8
    lane = lax.broadcasted_iota(jnp.int32, (8, width), 1)
    sub = lax.broadcasted_iota(jnp.int32, (8, width), 0)
    rows = [[strip[8 * t : 8 * t + 8] for t in range(tiles)] for strip in strips]
    pivots = [[None] * tiles for _ in strips]
    columns = [
        {k: {t: spread_lane(own[t], first + k) for t in range(tiles)} for k in range(AHEAD + 1)}
        for own in rows
    ]
    for j in range(STRIP):
        at, row = j // 8, j % 8
        below = sub > row
        here = lane == first + j
        for own, ahead, seen in zip(rows, columns, pivots):
            column = ahead.pop(j)
            pivot = spread_row(column[at], row)
            seen[at] = pivot if row == 0 else jnp.where(sub >= row, pivot, seen[at])
            inverse = pl.reciprocal(pivot, approx=True)
            factor = {t: column[t] for t in range(at + 1, tiles)}
            if row < 7:
                factor[at] = jnp.where(below, column[at], 0.0)
            for later in ahead.values():
                value = spread_row(later[at], row) * inverse
                for t in later:
                    if t in factor:
                        later[t] = later[t] - factor[t] * value
            pivot_row = jnp.where(here, 1.0, spread_row(own[at], row)) * inverse
            for t in factor:
                cleared = jnp.logical_and(here, below) if t == at else here
                own[t] = jnp.where(cleared, 0.0, own[t]) - factor[t] * pivot_row
            new = j + AHEAD + 1
            if new < STRIP:
                ahead[new] = {
                    t: spread_lane(own[t], first + new) for t in range((j + 1) // 8, tiles)
                }
    scaled = []
    for own, seen in zip(rows, pivots):
        out = []
        for t in range(tiles):
            offset = lane - first - 8 * t
            tile = jnp.where(offset == sub, 1.0, own[t])
            tile = jnp.where(jnp.logical_and(offset > sub, lane < first + STRIP), 0.0, tile)
            out.append(tile * lax.rsqrt(seen[t]))
        scaled.append(jnp.concatenate(out, 0))
    return scaled


def panel_inverses(panels):
    width = panels[0].shape[0]
    rest = list(panels)
    inverse_rows = [[] for _ in panels]
    for first in range(0, width, STRIP):
        past = first + STRIP
        strips = eliminate([one[:STRIP] for one in rest], first, width)
        lane = lax.broadcasted_iota(jnp.int32, (STRIP, width), 1)
        for m, strip in enumerate(strips):
            inverse_rows[m].append(jnp.where(lane < past, strip, 0.0))
            if past < width:
                update = dot3(strip, strip, 0, 0)[past:]
                below = rest[m][STRIP:]
                lanes = lax.broadcasted_iota(jnp.int32, below.shape, 1)
                done = jnp.logical_and(lanes >= first, lanes < past)
                rest[m] = jnp.where(done, 0.0, below) - update
    return [jnp.concatenate(parts, 0) for parts in inverse_rows]


def basis_kernel(*refs, count, bits):
    place, parts, bases = refs[0], refs[1 : 1 + 2 * count], refs[1 + 2 * count : 1 + 3 * count]
    held, grams = refs[1 + 3 * count : 1 + 4 * count], refs[1 + 4 * count : 1 + 5 * count]
    leaf = refs[1 + 5 * count]
    columns, rows = held[0].shape
    scale = math.sqrt(rows)
    half = columns // 2
    for m, source in enumerate(held):
        source[pl.ds(pl.multiple_of(place[0] * half, half), half), :] = parts[2 * m][...]
        source[pl.ds(pl.multiple_of(half - place[0] * half, half), half), :] = parts[2 * m + 1][...]
    for source, gram in zip(held, grams):
        value = source[...]
        gram[...] = dot3(value, value, 1, 1)
    share = bases[0].shape[0]
    index = sum(place[b] << b for b in range(bits - 1))
    leaf[...] = held[0][:, pl.ds(pl.multiple_of(index * share, share), share)]
    held = (leaf,) + tuple(held[1:])
    for start in range(0, columns, PANEL):
        own, after = slice(start, start + PANEL), slice(start + PANEL, columns)
        last = start + PANEL == columns
        inverses = panel_inverses([gram[own, own] for gram in grams])
        for inverse, source, gram, basis in zip(inverses, held, grams, bases):
            if not last:
                lower = dot3(gram[after, own], inverse, 1, 1)
                gram[after, after] = gram[after, after] - dot3(lower, lower, 1, 1)
            block = dot3(inverse, source[own, :], 1, 0)
            basis[:, own] = block.T * scale
            if not last:
                source[after, :] = source[after, :] - dot3(lower, block, 1, 0)


def bases_of(place, parts, share):
    count = len(parts) // 2
    columns, rows = 2 * parts[0].shape[0], parts[0].shape[1]
    bits = lax.axis_size("samples").bit_length() - 1
    shapes = [(share if m == 0 else rows, columns) for m in range(count)]
    return pl.pallas_call(
        functools.partial(basis_kernel, count=count, bits=bits),
        out_shape=[jax.ShapeDtypeStruct(shape, F32) for shape in shapes],
        in_specs=[SMEM] + [VMEM] * len(parts),
        out_specs=[VMEM] * count,
        scratch_shapes=[pltpu.VMEM((columns, rows), F32)] * count
        + [pltpu.VMEM((columns, columns), F32)] * count
        + [pltpu.VMEM((columns, share), F32)],
        compiler_params=pltpu.CompilerParams(vmem_limit_bytes=BASES_VMEM),
        name="bases",
    )(place, *parts)


def call(kernel, shapes, *operands, **static):
    return pl.pallas_call(
        functools.partial(kernel, **static),
        out_shape=[jax.ShapeDtypeStruct(shape, F32) for shape in shapes],
        in_specs=[SMEM] + [VMEM] * (len(operands) - 1),
        out_specs=[VMEM] * len(shapes),
        compiler_params=pltpu.CompilerParams(vmem_limit_bytes=SMALL_VMEM),
        name=kernel.__name__,
    )(*operands)


def pick(value, indices):
    count, width = value.shape
    lanes = lax.broadcasted_iota(jnp.int32, (width, indices.shape[1]), 0)
    chosen = (lanes == indices).astype(BF16)
    high = value.astype(BF16)
    rest = value - high.astype(F32)
    middle = rest.astype(BF16)
    low = (rest - middle.astype(F32)).astype(BF16)
    found = dot_of(jnp.concatenate([high, middle, low], 0), chosen, 1, 0)
    return found[:count] + (found[count : 2 * count] + found[2 * count :])


def ordered(first, second, swapped):
    return jnp.concatenate(
        [jnp.where(swapped, second, first), jnp.where(swapped, first, second)], 1
    )


def part(ref, index, size):
    return ref[pl.ds(pl.multiple_of(index * size, size), size), :]


def chunk_start(place, bits, other, columns):
    return sum((place[b] ^ other >> b & 1) * (columns >> b + 1) for b in range(bits))


def product_kernel(place, matrix, sketch, pivots, *refs, bits):
    own, other = refs[:2]
    tops = refs[2 : 2 + (1 << bits)]
    rows_held, sketch_held, turned, found, sent, sems = refs[2 + (1 << bits) :]
    leaf, half, columns = matrix.shape[0] // 2, own.shape[0], sketch.shape[1]
    rank = pivots.shape[2]
    sketch_copy = pltpu.make_async_copy(sketch, sketch_held, sems.at[2])
    sketch_copy.start()
    copies = []
    for step in range(2):
        rows = pl.ds(step * leaf, leaf)
        copies.append(pltpu.make_async_copy(matrix.at[rows], rows_held.at[rows], sems.at[step]))
        copies[-1].start()
    sketch_copy.wait()
    turned[...] = sketch_held[...].T
    second = place[0] == 1
    for step, copy in enumerate(copies):
        copy.wait()
        lanes = slice(step * leaf, step * leaf + leaf)
        value = dot_of(turned[...], rows_held[lanes, :], 1, 1)
        near, far = value[:half], value[half:]
        own[:, lanes] = jnp.where(second, far, near)
        other[:, lanes] = jnp.where(second, near, far)
        found[:, step * rank : step * rank + rank] = pick(value, pivots[step])
    sent[...] = pick(found[...], pivots[2])
    for x, top in enumerate(tops):
        size = top.shape[0]
        start = chunk_start(place, bits, x, columns)
        top[...] = sent[pl.ds(pl.multiple_of(start, size), size), :]


def product(place, matrix, sketch, pivots, bits):
    rows, depth = matrix.shape
    columns, rank = sketch.shape[1], pivots.shape[2]
    shapes = [(columns // 2, rows)] * 2 + [(columns >> bits, rank)] * (1 << bits)
    hbm = pl.BlockSpec(memory_space=pltpu.HBM)
    return pl.pallas_call(
        functools.partial(product_kernel, bits=bits),
        out_shape=[jax.ShapeDtypeStruct(shape, F32) for shape in shapes],
        in_specs=[SMEM, hbm, hbm, VMEM],
        out_specs=[VMEM] * len(shapes),
        scratch_shapes=[
            pltpu.VMEM(matrix.shape, BF16),
            pltpu.VMEM(sketch.shape, BF16),
            pltpu.VMEM((columns, depth), BF16),
            pltpu.VMEM((columns, 2 * rank), F32),
            pltpu.VMEM((columns, rank), F32),
            pltpu.SemaphoreType.DMA((3,)),
        ],
        compiler_params=pltpu.CompilerParams(vmem_limit_bytes=PRODUCT_VMEM),
        name="product",
    )(place, matrix, sketch, pivots)


def add_and_halve(place, held, came, own, other, *, bit):
    half = own.shape[0]
    own[...] = part(held, place[bit], half) + part(came, place[bit], half)
    other[...] = part(held, 1 - place[bit], half) + part(came, 1 - place[bit], half)


def add_and_part(place, held, came, own, other, *, bit):
    leaf = own.shape[1]
    for index, out in ((place[bit], own), (1 - place[bit], other)):
        lanes = pl.ds(pl.multiple_of(index * leaf, leaf), leaf)
        out[...] = held[:, lanes] + came[:, lanes]


def add_all(place, *refs):
    refs[-1][...] = sum(ref[...] for ref in refs[1:-1]) + refs[0][...]


def leaf_kernel(place, held, came, pivots, leaf, skeleton, *, bit):
    value = held[...] + came[...]
    leaf[...] = value
    skeleton[...] = pick(value, pivots[place[bit]])


def join_lanes(place, own, came, out, *, bit):
    out[...] = ordered(own[...], came[...], place[bit] == 1)


def join_rows(place, own, came, out, *, bit):
    half = own.shape[0]
    out[pl.ds(pl.multiple_of(place[bit] * half, half), half), :] = own[...]
    out[pl.ds(pl.multiple_of(half - place[bit] * half, half), half), :] = came[...]


def messages(position, node, top, first, second, count):
    rank = top.shape[1]
    root = position % (count // 2) == 0
    first[...] = jnp.where(root, top, node[:, :rank])
    second[...] = jnp.where(root, top, node[:, rank:])


def two_levels(place, own, next_1, next_2, next_3, upper, node, top, first, second, *, at, count):
    position, depth = place[at], count.bit_length() - 1
    odd = position % 2 == 1
    pair = position >> 1
    first_row = (1 << depth - 1) - 2
    mine = ordered(own[...], next_1[...], odd)
    theirs = ordered(next_2[...], next_3[...], odd)
    mine_top = pick(mine, upper[pl.ds(first_row + pair, 1), :])
    theirs_top = pick(theirs, upper[pl.ds(first_row + (pair ^ 1), 1), :])
    both = ordered(mine_top, theirs_top, pair % 2 == 1)
    chosen = jnp.where(odd, mine, both)
    raised = pick(both, upper[pl.ds((1 << depth - 2) - 2 + (position >> 2), 1), :])
    node[...] = chosen
    top[...] = raised
    messages(position, chosen, raised, first, second, count)


def one_level(place, own, came, before, upper, node, top, first, second, *, at, height, count):
    position, depth = place[at], count.bit_length() - 1
    both = ordered(own[...], came[...], (position >> height - 1) % 2 == 1)
    owner = position % (1 << height) == 1 << height - 1
    chosen = jnp.where(owner, both, before[...])
    row = (1 << depth - height) - 2 + (position >> height)
    raised = pick(both, upper[pl.ds(row, 1), :])
    node[...] = chosen
    top[...] = raised
    messages(position, chosen, raised, first, second, count)


def join_node(place, node, top, first, second, third, out, *, at, count, bit):
    root = place[at] % (count // 2) == 0
    right = place[at] == count // 2
    own_root = ordered(top[...], third[...], right)
    half = node.shape[0]
    mine = pl.ds(pl.multiple_of(place[bit] * half, half), half)
    theirs = pl.ds(pl.multiple_of(half - place[bit] * half, half), half)
    out[mine, :] = jnp.where(root, own_root, node[...])
    out[theirs, :] = ordered(first[...], second[...], right)


def exchange(block, other):
    count = lax.axis_size("samples")
    return lax.ppermute(block, "samples", [(s, s ^ other) for s in range(count)])


def swap(block, bit):
    return exchange(block, 1 << bit)


def climb(place, current, upper, at, bits):
    count, shares = lax.axis_size("rows"), lax.axis_size("samples")
    depth = count.bit_length() - 1
    wide, narrow = (current.shape[0], 2 * current.shape[1]), current.shape
    came = [
        lax.ppermute(current, "rows", [(d, d ^ step) for d in range(count)]) for step in (1, 2, 3)
    ]
    shapes = [wide, narrow, narrow, narrow]
    node, top, first, second = call(
        two_levels, shapes, place, current, *came, upper, at=at, count=count
    )
    for height in range(3, depth):
        partner = lax.ppermute(top, "rows", [(d, d ^ 1 << height - 1) for d in range(count)])
        node, top, first, second = call(
            one_level, shapes, place, top, partner, node, upper, at=at, height=height, count=count
        )
    bit = bits - 1
    far = count // 2
    across, other_side, along = [], [], []
    for d in range(count):
        for s in range(shares):
            source = d * shares + s
            turned = s ^ 1 << bit
            across.append((source, d * shares + turned))
            if d % far == 0:
                other_side.append((source, (d ^ far) * shares + turned))
                along.append((source, (d ^ far) * shares + s))
            else:
                other_side.append((source, d * shares + turned))
    axes = ("rows", "samples")
    first = lax.ppermute(first, axes, across)
    second = lax.ppermute(second, axes, other_side)
    third = lax.ppermute(top, axes, along)
    half = (2 * wide[0], wide[1])
    return call(
        join_node, [half], place, node, top, first, second, third, at=at, count=count, bit=bit
    )[0]


def on_device(matrix_block, sketch_matrix, local_pivots, upper_pivots):
    shares = lax.axis_size("samples")
    bits = shares.bit_length() - 1
    share, position = lax.axis_index("samples"), lax.axis_index("rows")
    place = jnp.stack([share >> b & 1 for b in range(bits)] + [position]).astype(jnp.int32)
    pivots = jnp.transpose(local_pivots, (1, 0, 2))
    rows, rank = matrix_block.shape[0], pivots.shape[2]

    own, other, *tops = product(place, matrix_block, sketch_matrix, pivots, bits)
    tops = tops[:1] + [exchange(top, x) for x, top in enumerate(tops) if x > 0]
    came = exchange(other, 1)
    own, came, tops = lax.optimization_barrier((own, came, tops))
    for bit in range(1, bits - 1):
        half = (own.shape[0] // 2, rows)
        own, other = call(add_and_halve, [half] * 2, place, own, came, bit=bit)
        came = swap(other, bit)
    last = bits - 1
    leaf_shape = (own.shape[0], rows // 2)
    own, other = call(add_and_part, [leaf_shape] * 2, place, own, came, bit=last)
    came = swap(other, last)

    top = call(add_all, [tops[0].shape], place, *tops)[0]
    node = climb(place, top, upper_pivots, bits, bits)

    leaf, skeleton = call(
        leaf_kernel, [leaf_shape, (leaf_shape[0], rank)], place, own, came, pivots, bit=last
    )
    skeleton_came = swap(skeleton, last)
    stacked = call(
        join_lanes, [(leaf_shape[0], 2 * rank)], place, skeleton, skeleton_came, bit=last
    )[0]
    held = [leaf, stacked, node]
    for bit in range(bits - 2, 0, -1):
        whole = (2 * held[0].shape[0], held[0].shape[1])
        held = [call(join_rows, [whole], place, one, swap(one, bit), bit=bit)[0] for one in held]
    parts = []
    for one in held:
        parts += [one, swap(one, 0)]
    return tuple(bases_of(place, parts, rows // shares))


def solution(mesh):
    in_specs = (P("rows", "samples"), P("samples", None), P("rows", None, None), P())
    out_specs = (P(("rows", "samples"), None), P("rows", None), P("rows", None))
    return jax.shard_map(
        on_device, mesh=mesh, in_specs=in_specs, out_specs=out_specs, check_vma=False
    )
```

```python
import functools
import math

import jax
import jax.numpy as jnp
from jax import lax
from jax.experimental import pallas as pl
from jax.experimental.pallas import tpu as pltpu
from jax.sharding import PartitionSpec as P

F32 = jnp.float32
BF16 = jnp.bfloat16
PANEL = 128
STRIP = 32
AHEAD = 5
PRODUCT_VMEM = 51 << 20
SMALL_VMEM = 12 << 20
BASES_VMEM = 24 << 20
VMEM = pl.BlockSpec(memory_space=pltpu.VMEM)
SMEM = pl.BlockSpec(memory_space=pltpu.SMEM)


def dot_of(left, right, left_dim, right_dim):
    return lax.dot_general(
        left, right, (((left_dim,), (right_dim,)), ((), ())), preferred_element_type=F32
    )


def halves(value):
    high = value.astype(BF16)
    return high, (value - high.astype(F32)).astype(BF16)


def dot3(left, right, left_dim, right_dim):
    left_high, left_low = halves(left)
    right_high, right_low = halves(right)
    cross = dot_of(left_high, right_low, left_dim, right_dim)
    cross += dot_of(left_low, right_high, left_dim, right_dim)
    return dot_of(left_high, right_high, left_dim, right_dim) + cross


def spread_row(tile, row):
    return jnp.broadcast_to(tile[row : row + 1], tile.shape)


def spread_lane(tile, lane):
    return jnp.broadcast_to(tile[:, lane : lane + 1], tile.shape)


def eliminate(strips, first, width):
    tiles = STRIP // 8
    lane = lax.broadcasted_iota(jnp.int32, (8, width), 1)
    sub = lax.broadcasted_iota(jnp.int32, (8, width), 0)
    rows = [[strip[8 * t : 8 * t + 8] for t in range(tiles)] for strip in strips]
    pivots = [[None] * tiles for _ in strips]
    columns = [
        {k: {t: spread_lane(own[t], first + k) for t in range(tiles)} for k in range(AHEAD + 1)}
        for own in rows
    ]
    for j in range(STRIP):
        at, row = j // 8, j % 8
        below = sub > row
        here = lane == first + j
        for own, ahead, seen in zip(rows, columns, pivots):
            column = ahead.pop(j)
            pivot = spread_row(column[at], row)
            seen[at] = pivot if row == 0 else jnp.where(sub >= row, pivot, seen[at])
            inverse = pl.reciprocal(pivot, approx=True)
            factor = {t: column[t] for t in range(at + 1, tiles)}
            if row < 7:
                factor[at] = jnp.where(below, column[at], 0.0)
            for later in ahead.values():
                value = spread_row(later[at], row) * inverse
                for t in later:
                    if t in factor:
                        later[t] = later[t] - factor[t] * value
            pivot_row = jnp.where(here, 1.0, spread_row(own[at], row)) * inverse
            for t in factor:
                cleared = jnp.logical_and(here, below) if t == at else here
                own[t] = jnp.where(cleared, 0.0, own[t]) - factor[t] * pivot_row
            new = j + AHEAD + 1
            if new < STRIP:
                ahead[new] = {
                    t: spread_lane(own[t], first + new) for t in range((j + 1) // 8, tiles)
                }
    scaled = []
    for own, seen in zip(rows, pivots):
        out = []
        for t in range(tiles):
            offset = lane - first - 8 * t
            tile = jnp.where(offset == sub, 1.0, own[t])
            tile = jnp.where(jnp.logical_and(offset > sub, lane < first + STRIP), 0.0, tile)
            out.append(tile * lax.rsqrt(seen[t]))
        scaled.append(jnp.concatenate(out, 0))
    return scaled


def panel_inverses(panels):
    width = panels[0].shape[0]
    rest = list(panels)
    inverse_rows = [[] for _ in panels]
    for first in range(0, width, STRIP):
        past = first + STRIP
        strips = eliminate([one[:STRIP] for one in rest], first, width)
        lane = lax.broadcasted_iota(jnp.int32, (STRIP, width), 1)
        for m, strip in enumerate(strips):
            inverse_rows[m].append(jnp.where(lane < past, strip, 0.0))
            if past < width:
                update = dot3(strip, strip, 0, 0)[past:]
                below = rest[m][STRIP:]
                lanes = lax.broadcasted_iota(jnp.int32, below.shape, 1)
                done = jnp.logical_and(lanes >= first, lanes < past)
                rest[m] = jnp.where(done, 0.0, below) - update
    return [jnp.concatenate(parts, 0) for parts in inverse_rows]


def basis_kernel(*refs, count, bits):
    place, parts, bases = refs[0], refs[1 : 1 + 2 * count], refs[1 + 2 * count : 1 + 3 * count]
    held, grams = refs[1 + 3 * count : 1 + 4 * count], refs[1 + 4 * count : 1 + 5 * count]
    leaf = refs[1 + 5 * count]
    columns, rows = held[0].shape
    scale = math.sqrt(rows)
    half = columns // 2
    for m, source in enumerate(held):
        source[pl.ds(pl.multiple_of(place[0] * half, half), half), :] = parts[2 * m][...]
        source[pl.ds(pl.multiple_of(half - place[0] * half, half), half), :] = parts[2 * m + 1][...]
    for source, gram in zip(held, grams):
        value = source[...]
        gram[...] = dot3(value, value, 1, 1)
    share = bases[0].shape[0]
    index = sum(place[b] << b for b in range(bits - 1))
    leaf[...] = held[0][:, pl.ds(pl.multiple_of(index * share, share), share)]
    held = (leaf,) + tuple(held[1:])
    for start in range(0, columns, PANEL):
        own, after = slice(start, start + PANEL), slice(start + PANEL, columns)
        last = start + PANEL == columns
        inverses = panel_inverses([gram[own, own] for gram in grams])
        for inverse, source, gram, basis in zip(inverses, held, grams, bases):
            if not last:
                lower = dot3(gram[after, own], inverse, 1, 1)
                gram[after, after] = gram[after, after] - dot3(lower, lower, 1, 1)
            block = dot3(inverse, source[own, :], 1, 0)
            basis[:, own] = block.T * scale
            if not last:
                source[after, :] = source[after, :] - dot3(lower, block, 1, 0)


def bases_of(place, parts, share):
    count = len(parts) // 2
    columns, rows = 2 * parts[0].shape[0], parts[0].shape[1]
    bits = lax.axis_size("samples").bit_length() - 1
    shapes = [(share if m == 0 else rows, columns) for m in range(count)]
    return pl.pallas_call(
        functools.partial(basis_kernel, count=count, bits=bits),
        out_shape=[jax.ShapeDtypeStruct(shape, F32) for shape in shapes],
        in_specs=[SMEM] + [VMEM] * len(parts),
        out_specs=[VMEM] * count,
        scratch_shapes=[pltpu.VMEM((columns, rows), F32)] * count
        + [pltpu.VMEM((columns, columns), F32)] * count
        + [pltpu.VMEM((columns, share), F32)],
        compiler_params=pltpu.CompilerParams(vmem_limit_bytes=BASES_VMEM),
        name="bases",
    )(place, *parts)


def call(kernel, shapes, *operands, **static):
    return pl.pallas_call(
        functools.partial(kernel, **static),
        out_shape=[jax.ShapeDtypeStruct(shape, F32) for shape in shapes],
        in_specs=[SMEM] + [VMEM] * (len(operands) - 1),
        out_specs=[VMEM] * len(shapes),
        compiler_params=pltpu.CompilerParams(vmem_limit_bytes=SMALL_VMEM),
        name=kernel.__name__,
    )(*operands)


def pick(value, indices):
    count, width = value.shape
    lanes = lax.broadcasted_iota(jnp.int32, (width, indices.shape[1]), 0)
    chosen = (lanes == indices).astype(BF16)
    high = value.astype(BF16)
    rest = value - high.astype(F32)
    middle = rest.astype(BF16)
    low = (rest - middle.astype(F32)).astype(BF16)
    found = dot_of(jnp.concatenate([high, middle, low], 0), chosen, 1, 0)
    return found[:count] + (found[count : 2 * count] + found[2 * count :])


def ordered(first, second, swapped):
    return jnp.concatenate(
        [jnp.where(swapped, second, first), jnp.where(swapped, first, second)], 1
    )


def part(ref, index, size):
    return ref[pl.ds(pl.multiple_of(index * size, size), size), :]


def chunk_start(place, bits, other, columns):
    return sum((place[b] ^ other >> b & 1) * (columns >> b + 1) for b in range(bits))


def product_kernel(place, matrix, sketch, pivots, *refs, bits):
    own, other = refs[:2]
    tops = refs[2 : 2 + (1 << bits)]
    rows_held, sketch_held, turned, found, sent, sems = refs[2 + (1 << bits) :]
    leaf, half, columns = matrix.shape[0] // 2, own.shape[0], sketch.shape[1]
    rank = pivots.shape[2]
    sketch_copy = pltpu.make_async_copy(sketch, sketch_held, sems.at[2])
    sketch_copy.start()
    copies = []
    for step in range(2):
        rows = pl.ds(step * leaf, leaf)
        copies.append(pltpu.make_async_copy(matrix.at[rows], rows_held.at[rows], sems.at[step]))
        copies[-1].start()
    sketch_copy.wait()
    turned[...] = sketch_held[...].T
    second = place[0] == 1
    for step, copy in enumerate(copies):
        copy.wait()
        lanes = slice(step * leaf, step * leaf + leaf)
        value = dot_of(turned[...], rows_held[lanes, :], 1, 1)
        near, far = value[:half], value[half:]
        own[:, lanes] = jnp.where(second, far, near)
        other[:, lanes] = jnp.where(second, near, far)
        found[:, step * rank : step * rank + rank] = pick(value, pivots[step])
    sent[...] = pick(found[...], pivots[2])
    for x, top in enumerate(tops):
        size = top.shape[0]
        start = chunk_start(place, bits, x, columns)
        top[...] = sent[pl.ds(pl.multiple_of(start, size), size), :]


def product(place, matrix, sketch, pivots, bits):
    rows, depth = matrix.shape
    columns, rank = sketch.shape[1], pivots.shape[2]
    shapes = [(columns // 2, rows)] * 2 + [(columns >> bits, rank)] * (1 << bits)
    hbm = pl.BlockSpec(memory_space=pltpu.HBM)
    return pl.pallas_call(
        functools.partial(product_kernel, bits=bits),
        out_shape=[jax.ShapeDtypeStruct(shape, F32) for shape in shapes],
        in_specs=[SMEM, hbm, hbm, VMEM],
        out_specs=[VMEM] * len(shapes),
        scratch_shapes=[
            pltpu.VMEM(matrix.shape, BF16),
            pltpu.VMEM(sketch.shape, BF16),
            pltpu.VMEM((columns, depth), BF16),
            pltpu.VMEM((columns, 2 * rank), F32),
            pltpu.VMEM((columns, rank), F32),
            pltpu.SemaphoreType.DMA((3,)),
        ],
        compiler_params=pltpu.CompilerParams(vmem_limit_bytes=PRODUCT_VMEM),
        name="product",
    )(place, matrix, sketch, pivots)


def add_and_halve(place, held, came, own, other, *, bit):
    half = own.shape[0]
    own[...] = part(held, place[bit], half) + part(came, place[bit], half)
    other[...] = part(held, 1 - place[bit], half) + part(came, 1 - place[bit], half)


def add_and_part(place, held, came, gate, own, other, *, bit):
    leaf = own.shape[1]
    for index, out in ((place[bit], own), (1 - place[bit], other)):
        lanes = pl.ds(pl.multiple_of(index * leaf, leaf), leaf)
        out[...] = held[:, lanes] + came[:, lanes]


def add_all(place, *refs):
    refs[-1][...] = sum(ref[...] for ref in refs[1:-1]) + refs[0][...]


def leaf_kernel(place, held, came, pivots, gate, leaf, skeleton, *, bit):
    value = held[...] + came[...]
    leaf[...] = value
    skeleton[...] = pick(value, pivots[place[bit]])


def join_lanes(place, own, came, out, *, bit):
    out[...] = ordered(own[...], came[...], place[bit] == 1)


def join_rows(place, own, came, out, *, bit):
    half = own.shape[0]
    out[pl.ds(pl.multiple_of(place[bit] * half, half), half), :] = own[...]
    out[pl.ds(pl.multiple_of(half - place[bit] * half, half), half), :] = came[...]


def messages(position, node, top, first, second, count):
    rank = top.shape[1]
    root = position % (count // 2) == 0
    first[...] = jnp.where(root, top, node[:, :rank])
    second[...] = jnp.where(root, top, node[:, rank:])


def two_levels(place, own, next_1, next_2, next_3, upper, node, top, first, second, *, at, count):
    position, depth = place[at], count.bit_length() - 1
    odd = position % 2 == 1
    pair = position >> 1
    first_row = (1 << depth - 1) - 2
    mine = ordered(own[...], next_1[...], odd)
    theirs = ordered(next_2[...], next_3[...], odd)
    mine_top = pick(mine, upper[pl.ds(first_row + pair, 1), :])
    theirs_top = pick(theirs, upper[pl.ds(first_row + (pair ^ 1), 1), :])
    both = ordered(mine_top, theirs_top, pair % 2 == 1)
    chosen = jnp.where(odd, mine, both)
    raised = pick(both, upper[pl.ds((1 << depth - 2) - 2 + (position >> 2), 1), :])
    node[...] = chosen
    top[...] = raised
    messages(position, chosen, raised, first, second, count)


def one_level(place, own, came, before, upper, node, top, first, second, *, at, height, count):
    position, depth = place[at], count.bit_length() - 1
    both = ordered(own[...], came[...], (position >> height - 1) % 2 == 1)
    owner = position % (1 << height) == 1 << height - 1
    chosen = jnp.where(owner, both, before[...])
    row = (1 << depth - height) - 2 + (position >> height)
    raised = pick(both, upper[pl.ds(row, 1), :])
    node[...] = chosen
    top[...] = raised
    messages(position, chosen, raised, first, second, count)


def join_node(place, node, top, first, second, third, out, *, at, count, bit):
    root = place[at] % (count // 2) == 0
    right = place[at] == count // 2
    own_root = ordered(top[...], third[...], right)
    half = node.shape[0]
    mine = pl.ds(pl.multiple_of(place[bit] * half, half), half)
    theirs = pl.ds(pl.multiple_of(half - place[bit] * half, half), half)
    out[mine, :] = jnp.where(root, own_root, node[...])
    out[theirs, :] = ordered(first[...], second[...], right)


def exchange(block, other):
    count = lax.axis_size("samples")
    return lax.ppermute(block, "samples", [(s, s ^ other) for s in range(count)])


def swap(block, bit):
    return exchange(block, 1 << bit)


def climb(place, current, upper, at, bits, aside):
    count, shares = lax.axis_size("rows"), lax.axis_size("samples")
    depth = count.bit_length() - 1
    wide, narrow = (current.shape[0], 2 * current.shape[1]), current.shape
    came = [
        lax.ppermute(current, "rows", [(d, d ^ step) for d in range(count)]) for step in (1, 2, 3)
    ]
    shapes = [wide, narrow, narrow, narrow]
    node, top, first, second = call(
        two_levels, shapes, place, current, *came, upper, at=at, count=count
    )
    for height in range(3, depth):
        partner = lax.ppermute(top, "rows", [(d, d ^ 1 << height - 1) for d in range(count)])
        node, top, first, second = call(
            one_level, shapes, place, top, partner, node, upper, at=at, height=height, count=count
        )
    bit = bits - 1
    far = count // 2
    across, other_side, along = [], [], []
    for d in range(count):
        for s in range(shares):
            source = d * shares + s
            turned = s ^ 1 << bit
            across.append((source, d * shares + turned))
            if d % far == 0:
                other_side.append((source, (d ^ far) * shares + turned))
                along.append((source, (d ^ far) * shares + s))
            else:
                other_side.append((source, d * shares + turned))
    axes = ("rows", "samples")
    first = lax.ppermute(first, axes, across)
    second = lax.ppermute(second, axes, other_side)
    third = lax.ppermute(top, axes, along)
    half = (2 * wide[0], wide[1])
    extra = aside(node)
    leaf_came = extra[-1]
    first, second, third, leaf_came = lax.optimization_barrier((first, second, third, leaf_came))
    joined = call(
        join_node, [half], place, node, top, first, second, third, at=at, count=count, bit=bit
    )[0]
    return joined, extra[:-1] + (leaf_came,)


def on_device(matrix_block, sketch_matrix, local_pivots, upper_pivots):
    shares = lax.axis_size("samples")
    bits = shares.bit_length() - 1
    share, position = lax.axis_index("samples"), lax.axis_index("rows")
    place = jnp.stack([share >> b & 1 for b in range(bits)] + [position]).astype(jnp.int32)
    pivots = jnp.transpose(local_pivots, (1, 0, 2))
    rows, rank = matrix_block.shape[0], pivots.shape[2]

    own, other, *tops = product(place, matrix_block, sketch_matrix, pivots, bits)
    tops = tops[:1] + [exchange(top, x) for x, top in enumerate(tops) if x > 0]
    came = exchange(other, 1)
    for bit in range(1, bits - 1):
        half = (own.shape[0] // 2, rows)
        own, other = call(add_and_halve, [half] * 2, place, own, came, bit=bit)
        came = swap(other, bit)
    top = call(add_all, [tops[0].shape], place, *tops)[0]
    last = bits - 1
    leaf_shape = (own.shape[0], rows // 2)
    own, other = call(add_and_part, [leaf_shape] * 2, place, own, came, top, bit=last)
    came = swap(other, last)

    def leaf_part(gate):
        leaf, skeleton = call(
            leaf_kernel,
            [leaf_shape, (leaf_shape[0], rank)],
            place, own, came, pivots, gate, bit=last,
        )
        return leaf, skeleton, swap(skeleton, last), exchange(leaf, 1)

    node, (leaf, skeleton, skeleton_came, leaf_came) = climb(
        place, top, upper_pivots, bits, bits, leaf_part
    )
    stacked = call(
        join_lanes, [(leaf_shape[0], 2 * rank)], place, skeleton, skeleton_came, bit=last
    )[0]
    held = [leaf, stacked, node]
    for bit in range(bits - 2, 0, -1):
        whole = (2 * held[0].shape[0], held[0].shape[1])
        held = [call(join_rows, [whole], place, one, swap(one, bit), bit=bit)[0] for one in held]
    came = [exchange(one, 1) for one in held]
    if bits == 2:
        came[0] = leaf_came
    parts = [half for pair in zip(held, came) for half in pair]
    return tuple(bases_of(place, parts, rows // shares))


def solution(mesh):
    in_specs = (P("rows", "samples"), P("samples", None), P("rows", None, None), P())
    out_specs = (P(("rows", "samples"), None), P("rows", None), P("rows", None))
    return jax.shard_map(
        on_device, mesh=mesh, in_specs=in_specs, out_specs=out_specs, check_vma=False
    )
```

```python
import functools
import math

import jax
import jax.numpy as jnp
from jax import lax
from jax.experimental import pallas as pl
from jax.experimental.pallas import tpu as pltpu
from jax.sharding import PartitionSpec as P

F32 = jnp.float32
BF16 = jnp.bfloat16
PANEL = 128
STRIP = 32
AHEAD = 4
PRODUCT_VMEM = 51 << 20
SMALL_VMEM = 12 << 20
BASES_VMEM = 24 << 20
VMEM = pl.BlockSpec(memory_space=pltpu.VMEM)
SMEM = pl.BlockSpec(memory_space=pltpu.SMEM)


def dot_of(left, right, left_dim, right_dim):
    return lax.dot_general(
        left, right, (((left_dim,), (right_dim,)), ((), ())), preferred_element_type=F32
    )


def halves(value):
    high = value.astype(BF16)
    return high, (value - high.astype(F32)).astype(BF16)


def dot3(left, right, left_dim, right_dim):
    left_high, left_low = halves(left)
    right_high, right_low = halves(right)
    cross = dot_of(left_high, right_low, left_dim, right_dim)
    cross += dot_of(left_low, right_high, left_dim, right_dim)
    return dot_of(left_high, right_high, left_dim, right_dim) + cross


def spread_row(tile, row):
    return jnp.broadcast_to(tile[row : row + 1], tile.shape)


def spread_lane(tile, lane):
    return jnp.broadcast_to(tile[:, lane : lane + 1], tile.shape)


def eliminate(strips, first, width, hold):
    tiles = STRIP // 8
    lane = lax.broadcasted_iota(jnp.int32, (8, width), 1)
    sub = lax.broadcasted_iota(jnp.int32, (8, width), 0)
    rows = [[strip[8 * t : 8 * t + 8] for t in range(tiles)] for strip in strips]
    pivots = [[None] * tiles for _ in strips]

    def spread_from(own, k):
        return {t: spread_lane(own[t], first + k) for t in range(k // 8, tiles)}

    columns = [{k: spread_from(own, k) for k in range(AHEAD + 1)} for own in rows]
    for j in range(STRIP):
        at, row, slot = j // 8, j % 8, j % hold.shape[1]
        below = sub > row
        here = lane == first + j
        for m, (own, ahead, seen) in enumerate(zip(rows, columns, pivots)):
            column = ahead.pop(j)
            pivot = spread_row(column[at], row)
            seen[at] = pivot if row == 0 else jnp.where(sub >= row, pivot, seen[at])
            inverse = pl.reciprocal(pivot, approx=True)
            for t in sorted({k // 8 for k in ahead if k > j + 1}):
                hold[m, slot, t] = column[t]
            hold[m, slot, tiles] = own[at]
            factor = {t: column[t] for t in range(at + 1, tiles)}
            if row < 7:
                factor[at] = jnp.where(below, column[at], 0.0)
            for k, later in ahead.items():
                if k == j + 1:
                    value = spread_row(column[k // 8], k % 8)
                else:
                    value = jnp.broadcast_to(hold[m, slot, k // 8, k % 8 : k % 8 + 1], (8, width))
                value = value * inverse
                for t in later:
                    if t in factor:
                        later[t] = later[t] - factor[t] * value
            pivot_row = jnp.broadcast_to(hold[m, slot, tiles, row : row + 1], (8, width))
            pivot_row = jnp.where(here, 1.0, pivot_row) * inverse
            for t in factor:
                cleared = jnp.logical_and(here, below) if t == at else here
                own[t] = jnp.where(cleared, 0.0, own[t]) - factor[t] * pivot_row
            new = j + AHEAD + 1
            if new < STRIP:
                ahead[new] = spread_from(own, new)
    scaled = []
    for own, seen in zip(rows, pivots):
        out = []
        for t in range(tiles):
            offset = lane - first - 8 * t
            tile = jnp.where(offset == sub, 1.0, own[t])
            tile = jnp.where(jnp.logical_and(offset > sub, lane < first + STRIP), 0.0, tile)
            out.append(tile * lax.rsqrt(seen[t]))
        scaled.append(jnp.concatenate(out, 0))
    return scaled


def panel_inverses(panels, hold):
    width = panels[0].shape[0]
    rest = list(panels)
    inverse_rows = [[] for _ in panels]
    for first in range(0, width, STRIP):
        past = first + STRIP
        strips = eliminate([one[:STRIP] for one in rest], first, width, hold)
        lane = lax.broadcasted_iota(jnp.int32, (STRIP, width), 1)
        for m, strip in enumerate(strips):
            inverse_rows[m].append(jnp.where(lane < past, strip, 0.0))
            if past < width:
                update = dot3(strip, strip, 0, 0)[past:]
                below = rest[m][STRIP:]
                lanes = lax.broadcasted_iota(jnp.int32, below.shape, 1)
                done = jnp.logical_and(lanes >= first, lanes < past)
                rest[m] = jnp.where(done, 0.0, below) - update
    return [jnp.concatenate(parts, 0) for parts in inverse_rows]


def basis_kernel(*refs, count, bits):
    place, own, came, *refs = refs
    bases, held, grams = refs[:count], refs[count : 2 * count], refs[2 * count : 3 * count]
    leaf, hold = refs[3 * count :]
    columns, rows = held[0].shape
    scale = math.sqrt(rows)
    half = columns // 2
    for m, source in enumerate(held):
        lanes = slice(m * rows, m * rows + rows)
        source[pl.ds(pl.multiple_of(place[0] * half, half), half), :] = own[:, lanes]
        source[pl.ds(pl.multiple_of(half - place[0] * half, half), half), :] = came[:, lanes]
    for source, gram in zip(held, grams):
        value = source[...]
        gram[...] = dot3(value, value, 1, 1)
    share = bases[0].shape[0]
    index = sum(place[b] << b for b in range(bits - 1))
    leaf[...] = held[0][:, pl.ds(pl.multiple_of(index * share, share), share)]
    held = (leaf,) + tuple(held[1:])
    for start in range(0, columns, PANEL):
        own, after = slice(start, start + PANEL), slice(start + PANEL, columns)
        last = start + PANEL == columns
        inverses = panel_inverses([gram[own, own] for gram in grams], hold)
        for inverse, source, gram, basis in zip(inverses, held, grams, bases):
            if not last:
                lower = dot3(gram[after, own], inverse, 1, 1)
                gram[after, after] = gram[after, after] - dot3(lower, lower, 1, 1)
            block = dot3(inverse, source[own, :], 1, 0)
            basis[:, own] = block.T * scale
            if not last:
                source[after, :] = source[after, :] - dot3(lower, block, 1, 0)


def bases_of(place, own, came, share):
    count = 3
    columns, rows = 2 * own.shape[0], own.shape[1] // count
    bits = lax.axis_size("samples").bit_length() - 1
    shapes = [(share if m == 0 else rows, columns) for m in range(count)]
    return pl.pallas_call(
        functools.partial(basis_kernel, count=count, bits=bits),
        out_shape=[jax.ShapeDtypeStruct(shape, F32) for shape in shapes],
        in_specs=[SMEM, VMEM, VMEM],
        out_specs=[VMEM] * count,
        scratch_shapes=[pltpu.VMEM((columns, rows), F32)] * count
        + [pltpu.VMEM((columns, columns), F32)] * count
        + [pltpu.VMEM((columns, share), F32), pltpu.VMEM((count, 4, STRIP // 8 + 1, 8, PANEL), F32)],
        compiler_params=pltpu.CompilerParams(vmem_limit_bytes=BASES_VMEM),
        name="bases",
    )(place, own, came)


def call(kernel, shapes, *operands, **static):
    return pl.pallas_call(
        functools.partial(kernel, **static),
        out_shape=[jax.ShapeDtypeStruct(shape, F32) for shape in shapes],
        in_specs=[SMEM] + [VMEM] * (len(operands) - 1),
        out_specs=[VMEM] * len(shapes),
        compiler_params=pltpu.CompilerParams(vmem_limit_bytes=SMALL_VMEM),
        name=kernel.__name__,
    )(*operands)


def pick(value, indices):
    count, width = value.shape
    lanes = lax.broadcasted_iota(jnp.int32, (width, indices.shape[1]), 0)
    chosen = (lanes == indices).astype(BF16)
    high = value.astype(BF16)
    rest = value - high.astype(F32)
    middle = rest.astype(BF16)
    low = (rest - middle.astype(F32)).astype(BF16)
    found = dot_of(jnp.concatenate([high, middle, low], 0), chosen, 1, 0)
    return found[:count] + (found[count : 2 * count] + found[2 * count :])


def ordered(first, second, swapped):
    return jnp.concatenate(
        [jnp.where(swapped, second, first), jnp.where(swapped, first, second)], 1
    )


def part(ref, index, size):
    return ref[pl.ds(pl.multiple_of(index * size, size), size), :]


def chunk_start(place, bits, other, columns):
    return sum((place[b] ^ other >> b & 1) * (columns >> b + 1) for b in range(bits))


def product_kernel(place, matrix, sketch, pivots, *refs, bits):
    own, other = refs[:2]
    tops = refs[2 : 2 + (1 << bits)]
    rows_held, sketch_held, turned, found, sent, sems = refs[2 + (1 << bits) :]
    leaf, half, columns = matrix.shape[0] // 2, own.shape[0], sketch.shape[1]
    rank = pivots.shape[2]
    sketch_copy = pltpu.make_async_copy(sketch, sketch_held, sems.at[2])
    sketch_copy.start()
    copies = []
    for step in range(2):
        rows = pl.ds(step * leaf, leaf)
        copies.append(pltpu.make_async_copy(matrix.at[rows], rows_held.at[rows], sems.at[step]))
        copies[-1].start()
    sketch_copy.wait()
    turned[...] = sketch_held[...].T
    second = place[0] == 1
    for step, copy in enumerate(copies):
        copy.wait()
        lanes = slice(step * leaf, step * leaf + leaf)
        value = dot_of(turned[...], rows_held[lanes, :], 1, 1)
        near, far = value[:half], value[half:]
        own[:, lanes] = jnp.where(second, far, near)
        other[:, lanes] = jnp.where(second, near, far)
        found[:, step * rank : step * rank + rank] = pick(value, pivots[step])
    sent[...] = pick(found[...], pivots[2])
    for x, top in enumerate(tops):
        size = top.shape[0]
        start = chunk_start(place, bits, x, columns)
        top[...] = sent[pl.ds(pl.multiple_of(start, size), size), :]


def product(place, matrix, sketch, pivots, bits):
    rows, depth = matrix.shape
    columns, rank = sketch.shape[1], pivots.shape[2]
    shapes = [(columns // 2, rows)] * 2 + [(columns >> bits, rank)] * (1 << bits)
    hbm = pl.BlockSpec(memory_space=pltpu.HBM)
    return pl.pallas_call(
        functools.partial(product_kernel, bits=bits),
        out_shape=[jax.ShapeDtypeStruct(shape, F32) for shape in shapes],
        in_specs=[SMEM, hbm, hbm, VMEM],
        out_specs=[VMEM] * len(shapes),
        scratch_shapes=[
            pltpu.VMEM(matrix.shape, BF16),
            pltpu.VMEM(sketch.shape, BF16),
            pltpu.VMEM((columns, depth), BF16),
            pltpu.VMEM((columns, 2 * rank), F32),
            pltpu.VMEM((columns, rank), F32),
            pltpu.SemaphoreType.DMA((3,)),
        ],
        compiler_params=pltpu.CompilerParams(vmem_limit_bytes=PRODUCT_VMEM),
        name="product",
    )(place, matrix, sketch, pivots)


def add_and_halve(place, held, came, own, other, *, bit):
    half = own.shape[0]
    own[...] = part(held, place[bit], half) + part(came, place[bit], half)
    other[...] = part(held, 1 - place[bit], half) + part(came, 1 - place[bit], half)


def add_and_part(place, held, came, pivots, gate, own, kept, sent, *, bit):
    leaf = own.shape[1]
    parts = []
    for index in (place[bit], 1 - place[bit]):
        lanes = pl.ds(pl.multiple_of(index * leaf, leaf), leaf)
        parts.append(held[:, lanes] + came[:, lanes])
    mine, theirs = parts
    own[...] = mine
    kept[...] = pick(theirs, pivots[1 - place[bit]])
    sent[:, :leaf] = theirs
    sent[:, leaf:] = pick(mine, pivots[place[bit]])


def add_all(place, *refs):
    refs[-1][...] = sum(ref[...] for ref in refs[1:-1]) + refs[0][...]


def join_rows(place, own, came, out, *, bit):
    half = own.shape[0]
    out[pl.ds(pl.multiple_of(place[bit] * half, half), half), :] = own[...]
    out[pl.ds(pl.multiple_of(half - place[bit] * half, half), half), :] = came[...]


def messages(position, node, top, first, second, count):
    rank = top.shape[1]
    root = position % (count // 2) == 0
    first[...] = jnp.where(root, top, node[:, :rank])
    second[...] = jnp.where(root, top, node[:, rank:])


def two_levels(place, own, next_1, next_2, next_3, upper, node, top, first, second, *, at, count):
    position, depth = place[at], count.bit_length() - 1
    odd = position % 2 == 1
    pair = position >> 1
    first_row = (1 << depth - 1) - 2
    mine = ordered(own[...], next_1[...], odd)
    theirs = ordered(next_2[...], next_3[...], odd)
    mine_top = pick(mine, upper[pl.ds(first_row + pair, 1), :])
    theirs_top = pick(theirs, upper[pl.ds(first_row + (pair ^ 1), 1), :])
    both = ordered(mine_top, theirs_top, pair % 2 == 1)
    chosen = jnp.where(odd, mine, both)
    raised = pick(both, upper[pl.ds((1 << depth - 2) - 2 + (position >> 2), 1), :])
    node[...] = chosen
    top[...] = raised
    messages(position, chosen, raised, first, second, count)


def one_level(place, own, came, before, upper, node, top, first, second, *, at, height, count):
    position, depth = place[at], count.bit_length() - 1
    both = ordered(own[...], came[...], (position >> height - 1) % 2 == 1)
    owner = position % (1 << height) == 1 << height - 1
    chosen = jnp.where(owner, both, before[...])
    row = (1 << depth - height) - 2 + (position >> height)
    raised = pick(both, upper[pl.ds(row, 1), :])
    node[...] = chosen
    top[...] = raised
    messages(position, chosen, raised, first, second, count)


def join_all(
    place, node, top, first, second, third, own, kept, came, pivots, out, *, at, count, bit
):
    leaf, rank = own.shape[1], kept.shape[1]
    value = own[...] + came[:, :leaf]
    out[:, :leaf] = value
    skeleton = pick(value, pivots[place[bit]])
    other = kept[...] + came[:, leaf:]
    out[:, leaf : leaf + 2 * rank] = ordered(skeleton, other, place[bit] == 1)
    root = place[at] % (count // 2) == 0
    right = place[at] == count // 2
    own_root = ordered(top[...], third[...], right)
    half = node.shape[0]
    mine = pl.ds(pl.multiple_of(place[bit] * half, half), half)
    theirs = pl.ds(pl.multiple_of(half - place[bit] * half, half), half)
    out[mine, leaf + 2 * rank :] = jnp.where(root, own_root, node[...])
    out[theirs, leaf + 2 * rank :] = ordered(first[...], second[...], right)


def exchange(block, other):
    count = lax.axis_size("samples")
    return lax.ppermute(block, "samples", [(s, s ^ other) for s in range(count)])


def swap(block, bit):
    return exchange(block, 1 << bit)


def climb(place, current, upper, at, bits):
    count, shares = lax.axis_size("rows"), lax.axis_size("samples")
    depth = count.bit_length() - 1
    wide, narrow = (current.shape[0], 2 * current.shape[1]), current.shape
    came = [
        lax.ppermute(current, "rows", [(d, d ^ step) for d in range(count)]) for step in (1, 2, 3)
    ]
    shapes = [wide, narrow, narrow, narrow]
    node, top, first, second = call(
        two_levels, shapes, place, current, *came, upper, at=at, count=count
    )
    for height in range(3, depth):
        partner = lax.ppermute(top, "rows", [(d, d ^ 1 << height - 1) for d in range(count)])
        node, top, first, second = call(
            one_level, shapes, place, top, partner, node, upper, at=at, height=height, count=count
        )
    bit = bits - 1
    far = count // 2
    across, other_side, along = [], [], []
    for d in range(count):
        for s in range(shares):
            source = d * shares + s
            turned = s ^ 1 << bit
            across.append((source, d * shares + turned))
            if d % far == 0:
                other_side.append((source, (d ^ far) * shares + turned))
                along.append((source, (d ^ far) * shares + s))
            else:
                other_side.append((source, d * shares + turned))
    axes = ("rows", "samples")
    first = lax.ppermute(first, axes, across)
    second = lax.ppermute(second, axes, other_side)
    third = lax.ppermute(top, axes, along)
    return node, top, first, second, third


def on_device(matrix_block, sketch_matrix, local_pivots, upper_pivots):
    shares = lax.axis_size("samples")
    bits = shares.bit_length() - 1
    share, position = lax.axis_index("samples"), lax.axis_index("rows")
    place = jnp.stack([share >> b & 1 for b in range(bits)] + [position]).astype(jnp.int32)
    pivots = jnp.transpose(local_pivots, (1, 0, 2))
    rows, rank = matrix_block.shape[0], pivots.shape[2]

    own, other, *tops = product(place, matrix_block, sketch_matrix, pivots, bits)
    tops = tops[:1] + [exchange(top, x) for x, top in enumerate(tops) if x > 0]
    came = exchange(other, 1)
    for bit in range(1, bits - 1):
        half = (own.shape[0] // 2, rows)
        own, other = call(add_and_halve, [half] * 2, place, own, came, bit=bit)
        came = swap(other, bit)
    top = call(add_all, [tops[0].shape], place, *tops)[0]
    last = bits - 1
    leaf_shape = (own.shape[0], rows // 2)
    sent_shape = (leaf_shape[0], leaf_shape[1] + rank)
    own, kept, sent = call(
        add_and_part,
        [leaf_shape, (leaf_shape[0], rank), sent_shape],
        place, own, came, pivots, top, bit=last,
    )
    came = swap(sent, last)
    node, top, *arrived = climb(place, top, upper_pivots, bits, bits)
    *arrived, came = lax.optimization_barrier((*arrived, came))
    held = call(
        join_all,
        [(leaf_shape[0], leaf_shape[1] + 4 * rank)],
        place, node, top, *arrived, own, kept, came, pivots, at=bits,
        count=lax.axis_size("rows"), bit=last,
    )[0]
    for bit in range(bits - 2, 0, -1):
        whole = (2 * held.shape[0], held.shape[1])
        held = call(join_rows, [whole], place, held, swap(held, bit), bit=bit)[0]
    return tuple(bases_of(place, held, exchange(held, 1), rows // shares))


def solution(mesh):
    in_specs = (P("rows", "samples"), P("samples", None), P("rows", None, None), P())
    out_specs = (P(("rows", "samples"), None), P("rows", None), P("rows", None))
    return jax.shard_map(
        on_device, mesh=mesh, in_specs=in_specs, out_specs=out_specs, check_vma=False
    )
```

```python
import functools
import math

import jax
import jax.numpy as jnp
from jax import lax
from jax.experimental import pallas as pl
from jax.experimental.pallas import tpu as pltpu
from jax.sharding import PartitionSpec as P

F32 = jnp.float32
BF16 = jnp.bfloat16
PANEL = 128
STRIP = 32
AHEAD = 4
PRODUCT_VMEM = 51 << 20
SMALL_VMEM = 12 << 20
BASES_VMEM = 24 << 20
VMEM = pl.BlockSpec(memory_space=pltpu.VMEM)
SMEM = pl.BlockSpec(memory_space=pltpu.SMEM)


def dot_of(left, right, left_dim, right_dim):
    return lax.dot_general(
        left, right, (((left_dim,), (right_dim,)), ((), ())), preferred_element_type=F32
    )


def halves(value):
    high = value.astype(BF16)
    return high, (value - high.astype(F32)).astype(BF16)


def dot3(left, right, left_dim, right_dim):
    left_high, left_low = halves(left)
    right_high, right_low = halves(right)
    cross = dot_of(left_high, right_low, left_dim, right_dim)
    cross += dot_of(left_low, right_high, left_dim, right_dim)
    return dot_of(left_high, right_high, left_dim, right_dim) + cross


def spread_row(tile, row):
    return jnp.broadcast_to(tile[row : row + 1], tile.shape)


def spread_lane(tile, lane):
    return jnp.broadcast_to(tile[:, lane : lane + 1], tile.shape)


def eliminate(strips, first, width, hold):
    tiles = STRIP // 8
    lane = lax.broadcasted_iota(jnp.int32, (8, width), 1)
    sub = lax.broadcasted_iota(jnp.int32, (8, width), 0)
    rows = [[strip[8 * t : 8 * t + 8] for t in range(tiles)] for strip in strips]
    pivots = [[None] * tiles for _ in strips]

    def spread_from(own, k):
        return {t: spread_lane(own[t], first + k) for t in range(k // 8, tiles)}

    columns = [{k: spread_from(own, k) for k in range(AHEAD + 1)} for own in rows]
    for j in range(STRIP):
        at, row, slot = j // 8, j % 8, j % hold.shape[1]
        below = sub > row
        here = lane == first + j
        for m, (own, ahead, seen) in enumerate(zip(rows, columns, pivots)):
            column = ahead.pop(j)
            pivot = spread_row(column[at], row)
            seen[at] = pivot if row == 0 else jnp.where(sub >= row, pivot, seen[at])
            inverse = pl.reciprocal(pivot, approx=True)
            for t in sorted({k // 8 for k in ahead if k > j + 1}):
                hold[m, slot, t] = column[t]
            hold[m, slot, tiles] = own[at]
            factor = {t: column[t] for t in range(at + 1, tiles)}
            if row < 7:
                factor[at] = jnp.where(below, column[at], 0.0)
            for k, later in ahead.items():
                if k == j + 1:
                    value = spread_row(column[k // 8], k % 8)
                else:
                    value = jnp.broadcast_to(hold[m, slot, k // 8, k % 8 : k % 8 + 1], (8, width))
                value = value * inverse
                for t in later:
                    if t in factor:
                        later[t] = later[t] - factor[t] * value
            pivot_row = jnp.broadcast_to(hold[m, slot, tiles, row : row + 1], (8, width))
            pivot_row = jnp.where(here, 1.0, pivot_row) * inverse
            for t in factor:
                cleared = jnp.logical_and(here, below) if t == at else here
                own[t] = jnp.where(cleared, 0.0, own[t]) - factor[t] * pivot_row
            new = j + AHEAD + 1
            if new < STRIP:
                ahead[new] = spread_from(own, new)
    scaled = []
    for own, seen in zip(rows, pivots):
        out = []
        for t in range(tiles):
            offset = lane - first - 8 * t
            tile = jnp.where(offset == sub, 1.0, own[t])
            tile = jnp.where(jnp.logical_and(offset > sub, lane < first + STRIP), 0.0, tile)
            out.append(tile * lax.rsqrt(seen[t]))
        scaled.append(jnp.concatenate(out, 0))
    return scaled


def panel_inverses(panels, hold):
    width = panels[0].shape[0]
    rest = list(panels)
    inverse_rows = [[] for _ in panels]
    for first in range(0, width, STRIP):
        past = first + STRIP
        strips = eliminate([one[:STRIP] for one in rest], first, width, hold)
        lane = lax.broadcasted_iota(jnp.int32, (STRIP, width), 1)
        for m, strip in enumerate(strips):
            inverse_rows[m].append(jnp.where(lane < past, strip, 0.0))
            if past < width:
                update = dot3(strip, strip, 0, 0)[past:]
                below = rest[m][STRIP:]
                lanes = lax.broadcasted_iota(jnp.int32, below.shape, 1)
                done = jnp.logical_and(lanes >= first, lanes < past)
                rest[m] = jnp.where(done, 0.0, below) - update
    return [jnp.concatenate(parts, 0) for parts in inverse_rows]


def basis_kernel(*refs, count, bits):
    place, own, came, *refs = refs
    bases, held, grams = refs[:count], refs[count : 2 * count], refs[2 * count : 3 * count]
    leaf, hold, *made, sems = refs[3 * count :]
    copies = []
    columns, rows = held[0].shape
    scale = math.sqrt(rows)
    half = columns // 2
    for m, source in enumerate(held):
        lanes = slice(m * rows, m * rows + rows)
        source[pl.ds(pl.multiple_of(place[0] * half, half), half), :] = own[:, lanes]
        source[pl.ds(pl.multiple_of(half - place[0] * half, half), half), :] = came[:, lanes]
    for source, gram in zip(held, grams):
        for start in range(0, columns, PANEL):
            own_rows = slice(start, start + PANEL)
            gram[start:, own_rows] = dot3(source[start:, :], source[own_rows, :], 1, 1)
    share = bases[0].shape[0]
    index = sum(place[b] << b for b in range(bits - 1))
    leaf[...] = held[0][:, pl.ds(pl.multiple_of(index * share, share), share)]
    held = (leaf,) + tuple(held[1:])
    for start in range(0, columns, PANEL):
        own, after = slice(start, start + PANEL), slice(start + PANEL, columns)
        last = start + PANEL == columns
        inverses = panel_inverses([gram[own, own] for gram in grams], hold)
        for m, (inverse, source, gram, basis) in enumerate(zip(inverses, held, grams, made)):
            if not last:
                lower = dot3(gram[after, own], inverse, 1, 1)
                for at in range(start + PANEL, columns, PANEL):
                    low = lower[at - start - PANEL :]
                    cut = slice(at, at + PANEL)
                    gram[at:, cut] = gram[at:, cut] - dot3(low, low[:PANEL], 1, 1)
            block = dot3(inverse, source[own, :], 1, 0)
            basis[:, own] = block.T * scale
            target = bases[m].at[:, own]
            copies.append(pltpu.make_async_copy(basis.at[:, own], target, sems.at[m, start // PANEL]))
            copies[-1].start()
            if not last:
                source[after, :] = source[after, :] - dot3(lower, block, 1, 0)
    for copy in copies:
        copy.wait()


def bases_of(place, own, came, share):
    count = 3
    columns, rows = 2 * own.shape[0], own.shape[1] // count
    bits = lax.axis_size("samples").bit_length() - 1
    shapes = [(share if m == 0 else rows, columns) for m in range(count)]
    return pl.pallas_call(
        functools.partial(basis_kernel, count=count, bits=bits),
        out_shape=[jax.ShapeDtypeStruct(shape, F32) for shape in shapes],
        in_specs=[SMEM, VMEM, VMEM],
        out_specs=[pl.BlockSpec(memory_space=pltpu.HBM)] * count,
        scratch_shapes=[pltpu.VMEM((columns, rows), F32)] * count
        + [pltpu.VMEM((columns, columns), F32)] * count
        + [pltpu.VMEM((columns, share), F32), pltpu.VMEM((count, 4, STRIP // 8 + 1, 8, PANEL), F32)]
        + [pltpu.VMEM(shape, F32) for shape in shapes]
        + [pltpu.SemaphoreType.DMA((count, columns // PANEL))],
        compiler_params=pltpu.CompilerParams(vmem_limit_bytes=BASES_VMEM),
        name="bases",
    )(place, own, came)


def call(kernel, shapes, *operands, **static):
    return pl.pallas_call(
        functools.partial(kernel, **static),
        out_shape=[jax.ShapeDtypeStruct(shape, F32) for shape in shapes],
        in_specs=[SMEM] + [VMEM] * (len(operands) - 1),
        out_specs=[VMEM] * len(shapes),
        compiler_params=pltpu.CompilerParams(vmem_limit_bytes=SMALL_VMEM),
        name=kernel.__name__,
    )(*operands)


def one_hot(indices, width):
    lanes = lax.broadcasted_iota(jnp.int32, (width, indices.shape[1]), 0)
    return (lanes == indices).astype(BF16)


def pick_by(value, chosen):
    count = value.shape[0]
    high = value.astype(BF16)
    rest = value - high.astype(F32)
    middle = rest.astype(BF16)
    low = (rest - middle.astype(F32)).astype(BF16)
    found = dot_of(jnp.concatenate([high, middle, low], 0), chosen, 1, 0)
    return found[:count] + (found[count : 2 * count] + found[2 * count :])


def pick(value, indices):
    return pick_by(value, one_hot(indices, value.shape[1]))


def ordered(first, second, swapped):
    return jnp.concatenate(
        [jnp.where(swapped, second, first), jnp.where(swapped, first, second)], 1
    )


def part(ref, index, size):
    return ref[pl.ds(pl.multiple_of(index * size, size), size), :]


def chunk_start(place, bits, other, columns):
    return sum((place[b] ^ other >> b & 1) * (columns >> b + 1) for b in range(bits))


def product_kernel(place, matrix, sketch, pivots, *refs, bits):
    own, other = refs[:2]
    tops = refs[2 : 2 + (1 << bits)]
    rows_held, sketch_held, turned, sent, chosen, sems = refs[2 + (1 << bits) :]
    leaf, half, columns = matrix.shape[0] // 2, own.shape[0], sketch.shape[1]
    rank = pivots.shape[2]
    sketch_copy = pltpu.make_async_copy(sketch, sketch_held, sems.at[2])
    sketch_copy.start()
    pivots_copy = pltpu.make_async_copy(pivots, chosen, sems.at[3])
    pivots_copy.start()
    copies = []
    for step in range(2):
        rows = pl.ds(step * leaf, leaf)
        copies.append(pltpu.make_async_copy(matrix.at[rows], rows_held.at[rows], sems.at[step]))
        copies[-1].start()
    pivots_copy.wait()
    last = one_hot(chosen[2], 2 * rank)
    both = [
        dot_of(one_hot(chosen[n], leaf), last[n * rank : n * rank + rank], 1, 0).astype(BF16)
        for n in range(2)
    ]
    sketch_copy.wait()
    turned[...] = sketch_held[...].T
    second = place[0] == 1
    picked = None
    for step, copy in enumerate(copies):
        copy.wait()
        lanes = slice(step * leaf, step * leaf + leaf)
        value = dot_of(turned[...], rows_held[lanes, :], 1, 1)
        near, far = value[:half], value[half:]
        own[:, lanes] = jnp.where(second, far, near)
        other[:, lanes] = jnp.where(second, near, far)
        found = pick_by(value, both[step])
        picked = found if picked is None else picked + found
    sent[...] = picked
    for x, top in enumerate(tops):
        size = top.shape[0]
        start = chunk_start(place, bits, x, columns)
        top[...] = sent[pl.ds(pl.multiple_of(start, size), size), :]


def product(place, matrix, sketch, pivots, bits):
    rows, depth = matrix.shape
    columns, rank = sketch.shape[1], pivots.shape[2]
    shapes = [(columns // 2, rows)] * 2 + [(columns >> bits, rank)] * (1 << bits)
    hbm = pl.BlockSpec(memory_space=pltpu.HBM)
    return pl.pallas_call(
        functools.partial(product_kernel, bits=bits),
        out_shape=[jax.ShapeDtypeStruct(shape, F32) for shape in shapes],
        in_specs=[SMEM, hbm, hbm, hbm],
        out_specs=[VMEM] * len(shapes),
        scratch_shapes=[
            pltpu.VMEM(matrix.shape, BF16),
            pltpu.VMEM(sketch.shape, BF16),
            pltpu.VMEM((columns, depth), BF16),
            pltpu.VMEM((columns, rank), F32),
            pltpu.VMEM(pivots.shape, jnp.int32),
            pltpu.SemaphoreType.DMA((4,)),
        ],
        compiler_params=pltpu.CompilerParams(vmem_limit_bytes=PRODUCT_VMEM),
        name="product",
    )(place, matrix, sketch, pivots)


def add_and_halve(place, held, came, own, other, *, bit):
    half = own.shape[0]
    own[...] = part(held, place[bit], half) + part(came, place[bit], half)
    other[...] = part(held, 1 - place[bit], half) + part(came, 1 - place[bit], half)


def add_and_part(place, held, came, pivots, *refs, bit):
    own, kept, sent = refs[-3:]
    leaf = own.shape[1]
    parts = []
    for index in (place[bit], 1 - place[bit]):
        lanes = pl.ds(pl.multiple_of(index * leaf, leaf), leaf)
        parts.append(held[:, lanes] + came[:, lanes])
    mine, theirs = parts
    own[...] = mine
    kept[...] = pick(theirs, pivots[1 - place[bit]])
    sent[:, :leaf] = theirs
    sent[:, leaf:] = pick(mine, pivots[place[bit]])


def add_all(place, *refs):
    refs[-1][...] = sum(ref[...] for ref in refs[1:-1]) + refs[0][...]


def join_rows(place, own, came, out, *, bit):
    half = own.shape[0]
    out[pl.ds(pl.multiple_of(place[bit] * half, half), half), :] = own[...]
    out[pl.ds(pl.multiple_of(half - place[bit] * half, half), half), :] = came[...]


def messages(position, node, top, first, second, count):
    rank = top.shape[1]
    root = position % (count // 2) == 0
    first[...] = jnp.where(root, top, node[:, :rank])
    second[...] = jnp.where(root, top, node[:, rank:])


def two_levels(place, own, next_1, next_2, next_3, upper, node, top, first, second, *, at, count):
    position, depth = place[at], count.bit_length() - 1
    odd = position % 2 == 1
    pair = position >> 1
    first_row = (1 << depth - 1) - 2
    mine = ordered(own[...], next_1[...], odd)
    theirs = ordered(next_2[...], next_3[...], odd)
    mine_top = pick(mine, upper[pl.ds(first_row + pair, 1), :])
    theirs_top = pick(theirs, upper[pl.ds(first_row + (pair ^ 1), 1), :])
    both = ordered(mine_top, theirs_top, pair % 2 == 1)
    chosen = jnp.where(odd, mine, both)
    raised = pick(both, upper[pl.ds((1 << depth - 2) - 2 + (position >> 2), 1), :])
    node[...] = chosen
    top[...] = raised
    messages(position, chosen, raised, first, second, count)


def one_level(place, own, came, before, upper, node, top, first, second, *, at, height, count):
    position, depth = place[at], count.bit_length() - 1
    both = ordered(own[...], came[...], (position >> height - 1) % 2 == 1)
    owner = position % (1 << height) == 1 << height - 1
    chosen = jnp.where(owner, both, before[...])
    row = (1 << depth - height) - 2 + (position >> height)
    raised = pick(both, upper[pl.ds(row, 1), :])
    node[...] = chosen
    top[...] = raised
    messages(position, chosen, raised, first, second, count)


def join_all(
    place, node, top, first, second, third, own, kept, came, pivots, out, *, at, count, bit
):
    leaf, rank = own.shape[1], kept.shape[1]
    value = own[...] + came[:, :leaf]
    out[:, :leaf] = value
    skeleton = pick(value, pivots[place[bit]])
    other = kept[...] + came[:, leaf:]
    out[:, leaf : leaf + 2 * rank] = ordered(skeleton, other, place[bit] == 1)
    root = place[at] % (count // 2) == 0
    right = place[at] == count // 2
    own_root = ordered(top[...], third[...], right)
    half = node.shape[0]
    mine = pl.ds(pl.multiple_of(place[bit] * half, half), half)
    theirs = pl.ds(pl.multiple_of(half - place[bit] * half, half), half)
    out[mine, leaf + 2 * rank :] = jnp.where(root, own_root, node[...])
    out[theirs, leaf + 2 * rank :] = ordered(first[...], second[...], right)


def exchange(block, other):
    count = lax.axis_size("samples")
    return lax.ppermute(block, "samples", [(s, s ^ other) for s in range(count)])


def swap(block, bit):
    return exchange(block, 1 << bit)


def climb(place, current, upper, at, bits):
    count, shares = lax.axis_size("rows"), lax.axis_size("samples")
    depth = count.bit_length() - 1
    wide, narrow = (current.shape[0], 2 * current.shape[1]), current.shape
    came = [
        lax.ppermute(current, "rows", [(d, d ^ step) for d in range(count)]) for step in (1, 2, 3)
    ]
    shapes = [wide, narrow, narrow, narrow]
    node, top, first, second = call(
        two_levels, shapes, place, current, *came, upper, at=at, count=count
    )
    for height in range(3, depth):
        partner = lax.ppermute(top, "rows", [(d, d ^ 1 << height - 1) for d in range(count)])
        node, top, first, second = call(
            one_level, shapes, place, top, partner, node, upper, at=at, height=height, count=count
        )
    bit = bits - 1
    far = count // 2
    across, other_side, along = [], [], []
    for d in range(count):
        for s in range(shares):
            source = d * shares + s
            turned = s ^ 1 << bit
            across.append((source, d * shares + turned))
            if d % far == 0:
                other_side.append((source, (d ^ far) * shares + turned))
                along.append((source, (d ^ far) * shares + s))
            else:
                other_side.append((source, d * shares + turned))
    axes = ("rows", "samples")
    first = lax.ppermute(first, axes, across)
    second = lax.ppermute(second, axes, other_side)
    third = lax.ppermute(top, axes, along)
    return node, top, first, second, third


def on_device(matrix_block, sketch_matrix, local_pivots, upper_pivots):
    shares = lax.axis_size("samples")
    bits = shares.bit_length() - 1
    share, position = lax.axis_index("samples"), lax.axis_index("rows")
    place = jnp.stack([share >> b & 1 for b in range(bits)] + [position]).astype(jnp.int32)
    pivots = jnp.transpose(local_pivots, (1, 0, 2))
    rows, rank = matrix_block.shape[0], pivots.shape[2]

    own, other, *tops = product(place, matrix_block, sketch_matrix, pivots, bits)
    tops = tops[:1] + [exchange(top, x) for x, top in enumerate(tops) if x > 0]
    came = exchange(other, 1)
    for bit in range(1, bits - 1):
        half = (own.shape[0] // 2, rows)
        own, other = call(add_and_halve, [half] * 2, place, own, came, bit=bit)
        came = swap(other, bit)
    top = call(add_all, [tops[0].shape], place, *tops)[0]
    last = bits - 1
    leaf_shape = (own.shape[0], rows // 2)
    sent_shape = (leaf_shape[0], leaf_shape[1] + rank)
    own, kept, sent = call(
        add_and_part,
        [leaf_shape, (leaf_shape[0], rank), sent_shape],
        place, own, came, pivots, top, bit=last,
    )
    came = swap(sent, last)
    node, top, *arrived = climb(place, top, upper_pivots, bits, bits)
    *arrived, came = lax.optimization_barrier((*arrived, came))
    held = call(
        join_all,
        [(leaf_shape[0], leaf_shape[1] + 4 * rank)],
        place, node, top, *arrived, own, kept, came, pivots, at=bits,
        count=lax.axis_size("rows"), bit=last,
    )[0]
    for bit in range(bits - 2, 0, -1):
        whole = (2 * held.shape[0], held.shape[1])
        held = call(join_rows, [whole], place, held, swap(held, bit), bit=bit)[0]
    return tuple(bases_of(place, held, exchange(held, 1), rows // shares))


def solution(mesh):
    in_specs = (P("rows", "samples"), P("samples", None), P("rows", None, None), P())
    out_specs = (P(("rows", "samples"), None), P("rows", None), P("rows", None))
    return jax.shard_map(
        on_device, mesh=mesh, in_specs=in_specs, out_specs=out_specs, check_vma=False
    )
```
